32 devices in a mesh: store: 8 (over y, x, core), ctx: 4 (over z).
Axes of the slice: x: 2, y: 2, z: 4, core: 2. Of those that a mesh axis runs over, the one named last changes fastest.
Arguments:
- tokens: bfloat16 [1024, 8192], P('store'), may hold values from -6 to 6
- joined_weight: bfloat16 [8192, 8, 1280], P(None, 'ctx'), may hold values from -0.0625 to 0.0625
- down_weight: bfloat16 [64, 8192, 64], P('store', 'ctx'), may hold values from -0.0625 to 0.0625
- up_weight: bfloat16 [64, 64, 8, 1280], P('store', None, 'ctx'), may hold values from -0.75 to 0.75
- adapter_per_request: int32 [1024], replicated, may hold values from 0 to 63, as said below
- adapter_store_slot: int32 [64], replicated, may hold values from 0 to 63, as said below
- prefix_block_list: int32 [1024, 4], P('store'), may hold values from 0 to 63, as said below
- prefix_length: int32 [1024], P('store'), may hold values from 1 to 64, as said below
- key_value_pool: bfloat16 [1024, 8, 256], P(('store', 'ctx')), may hold values from -400 to 400
Outputs:
- attn: bfloat16 [1024, 8, 1024], P('store', 'ctx')
The draws below stay inside these ranges and needn't reach their ends.
Inputs may be any that keep to these rules, and one draw needn't show every extreme that they name: `adapter_store_slot`: A permutation; slot s belongs to owner s // 8, which holds slots in store order. `adapter_per_request`: among the 128 requests of one store shard, at most 16 use adapters of one owner; on every shard one owner, the same for all shards, receives exactly 16. `prefix_block_list`: the 4 blocks of a request are distinct and lie in its store shard's range of 8 blocks, rows i * 128 to (i+1) * 128 - 1 using blocks i * 8 to (i+1) * 8 - 1. `prefix_length`: every store shard has a request of length 64.
All inputs are finite; a program needn't handle non-finite values.
Results may differ from the reference program's by a relative error of at most 0.02.
The reference program's roundings to bfloat16 on the way count: a program that leaves them out, or rounds other values in their place, can miss the bound.
Values may be sent and summed in bfloat16 or wider, within the bound.
A program may use at most 192 MiB of HBM per device.

```python
import jax
import jax.numpy as jnp
from jax import lax

MODEL_WIDTH = 8192
KEY_VALUE_HEADS = 8
QUERY_PER_KEY = 8
HEAD_SIZE = 128
ADAPTER_RANK = 64
CAP = 16
BLK = 16
SHARD_REQUESTS = 128
ADP_DEV = 8
REQUEST_COUNT = 1024
ADAPTER_COUNT = 64
GROUP_BLK = 8
MAXB = 4
MAXLEN = 64
PREFIX_TOKENS = 1024
JOINED_COLUMNS = 1280


def route_helper(key):
    shards = REQUEST_COUNT // SHARD_REQUESTS
    slot_of_adapter = jax.random.permutation(jax.random.fold_in(key, 11), ADAPTER_COUNT).astype(jnp.int32)
    adapter_of_slot = jnp.argsort(slot_of_adapter, stable=True).astype(jnp.int32)
    hot = jax.random.randint(jax.random.fold_in(key, 12), (), 0, shards)

    def one_shard(shard_key):
        initial_part, second, third = jax.random.split(shard_key, 3)
        positions = jnp.arange(shards * CAP, dtype=jnp.int32)
        ranks = jax.random.permutation(initial_part, shards * CAP).astype(jnp.int32) + CAP
        ranks = jnp.where(positions // CAP == hot, positions % CAP, ranks)
        chosen = jnp.argsort(ranks, stable=True)[:SHARD_REQUESTS].astype(jnp.int32)
        chosen = jax.random.permutation(second, chosen)
        owners = chosen // CAP
        local = jax.random.randint(third, (SHARD_REQUESTS,), 0, ADP_DEV)
        return adapter_of_slot[owners * ADP_DEV + local]
    keys = jax.random.split(jax.random.fold_in(key, 13), shards)
    request = jax.vmap(one_shard)(keys).reshape(REQUEST_COUNT)
    return (request.astype(jnp.int32), slot_of_adapter)


def draw_adapter_per_request(key, part):
    return route_helper(key)[0]


def draw_adapter_store_slot(key, part):
    return route_helper(key)[1]


def draw_prefix_block_list(key, part):
    keys = jax.random.split(key, REQUEST_COUNT)
    rows = jax.vmap(lambda row_key: jax.random.permutation(row_key, GROUP_BLK)[:MAXB])(keys)
    drawn_projection = jnp.arange(REQUEST_COUNT, dtype=jnp.int32) // SHARD_REQUESTS * GROUP_BLK
    return (rows.astype(jnp.int32) + drawn_projection[:, None]).astype(jnp.int32)


def draw_prefix_length(key, part):
    shards = REQUEST_COUNT // SHARD_REQUESTS
    initial_part, second = jax.random.split(key)
    lens = jax.random.randint(initial_part, (REQUEST_COUNT,), 1, MAXLEN + 1)
    where_long = jax.random.randint(second, (shards,), 0, SHARD_REQUESTS)
    index = jnp.arange(REQUEST_COUNT, dtype=jnp.int32)
    longest = index % SHARD_REQUESTS == jnp.repeat(where_long, SHARD_REQUESTS)
    return jnp.where(longest, MAXLEN, lens).astype(jnp.int32)


def draw_key_value_pool(key, part):
    initial_part = jax.random.fold_in(key, 0)
    value_rows = jnp.clip(jax.random.normal(initial_part, (PREFIX_TOKENS, KEY_VALUE_HEADS, 2 * HEAD_SIZE), jnp.float32), -6.0, 6.0)
    return value_rows.astype(jnp.bfloat16)


def steps_of(rng, dims, cuts, smallest, largest):
    loudness = 1.0
    for axis_at, parts in cuts:
        draws = jax.random.uniform(jax.random.fold_in(jax.random.fold_in(rng, 6), axis_at), (parts,), jnp.float32, smallest / len(cuts), largest / len(cuts))
        loudness = loudness * jnp.repeat(jnp.exp(draws), dims[axis_at] // parts).reshape((-1,) + (1,) * (len(dims) - 1 - axis_at))
    return loudness


def normal_values(key, shape, width, bound, cuts=(), kind=jnp.bfloat16):
    loudness = steps_of(key, shape, cuts, -0.22, 0.18) if cuts else 1.0
    drawn = jax.random.normal(key, shape, jnp.float32) * width * loudness
    return jnp.minimum(jnp.maximum(drawn, -bound), bound).astype(kind)


def setup_inputs(seed: int = 0) -> dict:
    seeds = jax.random.split(jax.random.key(seed), 10)
    tokens = normal_values(seeds[0], (REQUEST_COUNT, MODEL_WIDTH), 1.0, 6.0, ((0, 8),))
    joined_weight = normal_values(seeds[1], (MODEL_WIDTH, KEY_VALUE_HEADS, JOINED_COLUMNS), MODEL_WIDTH ** -0.5, 0.0625, ((1, 4),))
    down_weight = normal_values(seeds[2], (ADAPTER_COUNT, MODEL_WIDTH, ADAPTER_RANK), MODEL_WIDTH ** -0.5, 0.0625, ((0, 8), (1, 4)))
    up_weight = normal_values(seeds[3], (ADAPTER_COUNT, ADAPTER_RANK, KEY_VALUE_HEADS, JOINED_COLUMNS), ADAPTER_RANK ** -0.5, 0.75, ((0, 8), (2, 4)))
    adapter_per_request = draw_adapter_per_request(jax.random.fold_in(seeds[9], 71), 0)
    adapter_store_slot = draw_adapter_store_slot(jax.random.fold_in(seeds[9], 71), 0)
    prefix_block_list = draw_prefix_block_list(jax.random.fold_in(seeds[9], 71), 0)
    prefix_length = draw_prefix_length(jax.random.fold_in(seeds[9], 71), 0)
    key_value_pool = draw_key_value_pool(jax.random.fold_in(seeds[9], 71), 0)
    return {"tokens": tokens, "joined_weight": joined_weight, "down_weight": down_weight, "up_weight": up_weight, "adapter_per_request": adapter_per_request, "adapter_store_slot": adapter_store_slot, "prefix_block_list": prefix_block_list, "prefix_length": prefix_length, "key_value_pool": key_value_pool}


ROPE_THETA = 500000.0
ADAPTER_SCALE = 2.0


def rotary_apply(vec, token_position):
    half = vec.shape[-1] // 2
    freq = jnp.power(ROPE_THETA, -(jnp.arange(half, dtype=jnp.float32) * 2.0 / vec.shape[-1]))
    angle = token_position[..., None] * freq
    cosine = jnp.cos(angle)
    sine = jnp.sin(angle)
    initial_part = vec[..., :half]
    second = vec[..., half:]
    return jnp.concatenate([initial_part * cosine - second * sine, initial_part * sine + second * cosine], axis=-1)


def prefix_mask(local_ids, lens, group_blocks, blk):
    listed = local_ids.shape[1]
    equal = local_ids[:, :, None] == jnp.arange(group_blocks, dtype=jnp.int32)[None, None, :]
    start = jnp.sum(jnp.where(equal, (jnp.arange(listed, dtype=jnp.int32) * blk)[None, :, None], 0), axis=1)
    present = jnp.any(equal, axis=1)
    offset = jnp.arange(blk, dtype=jnp.int32)
    live = present[:, :, None] & (start[:, :, None] + offset[None, None, :] < lens[:, None, None])
    return live.reshape(local_ids.shape[0], group_blocks * blk)


def attend(query_rows, key_new, value_new, keys, value_rows, live):
    scale = 1.0 / (HEAD_SIZE ** 0.5)
    pool_scores = jnp.einsum('rhgd,thd->rhgt', query_rows.astype(jnp.float32), keys.astype(jnp.float32)) * scale
    own = jnp.einsum('rhgd,rhd->rhg', query_rows.astype(jnp.float32), key_new.astype(jnp.float32)) * scale
    mask = live[:, None, None, :]
    pool_scores = jnp.where(mask, pool_scores, -jnp.inf)
    top = jnp.maximum(jnp.max(pool_scores, axis=-1), own)
    prob = jnp.where(mask, jnp.exp(pool_scores - top[..., None]), 0.0)
    prob_own = jnp.exp(own - top)
    total = jnp.sum(prob, axis=-1) + prob_own
    prob_low = prob.astype(jnp.bfloat16)
    own_low = prob_own.astype(jnp.bfloat16)
    mixed = jnp.einsum('rhgt,thd->rhgd', prob_low.astype(jnp.float32), value_rows.astype(jnp.float32))
    mixed = mixed + own_low.astype(jnp.float32)[..., None] * value_new.astype(jnp.float32)[:, :, None, :]
    mixed = mixed / total[..., None]
    return mixed.astype(jnp.bfloat16).reshape(query_rows.shape[0], query_rows.shape[1], -1)


def reference(tokens, joined_weight, down_weight, up_weight, adapter_per_request, adapter_store_slot, prefix_block_list, prefix_length, key_value_pool):
    group_tokens = GROUP_BLK * BLK
    weight_flattened = joined_weight.reshape(MODEL_WIDTH, KEY_VALUE_HEADS * JOINED_COLUMNS)

    def one_shard(args):
        input_rows, adapters, lens, ids, shard = args
        store_slot = adapter_store_slot[adapters]
        down_picked = down_weight[store_slot].astype(jnp.float32)
        shrunk = jnp.einsum('rd,rdk->rk', input_rows.astype(jnp.float32), down_picked).astype(jnp.bfloat16)
        up_picked = up_weight[store_slot].astype(jnp.float32)
        adapter_update = jnp.einsum('rk,rkhc->rhc', shrunk.astype(jnp.float32), up_picked).astype(jnp.bfloat16)
        plain_projection = jnp.dot(input_rows, weight_flattened, preferred_element_type=jnp.float32).reshape(SHARD_REQUESTS, KEY_VALUE_HEADS, JOINED_COLUMNS)
        joined_projection = plain_projection + ADAPTER_SCALE * adapter_update.astype(jnp.float32)
        token_position = lens.astype(jnp.float32)
        query_rows = rotary_apply(joined_projection[:, :, :QUERY_PER_KEY * HEAD_SIZE].reshape(SHARD_REQUESTS, KEY_VALUE_HEADS, QUERY_PER_KEY, HEAD_SIZE), token_position[:, None, None]).astype(jnp.bfloat16)
        key_new = rotary_apply(joined_projection[:, :, QUERY_PER_KEY * HEAD_SIZE:(QUERY_PER_KEY + 1) * HEAD_SIZE], token_position[:, None]).astype(jnp.bfloat16)
        value_new = joined_projection[:, :, (QUERY_PER_KEY + 1) * HEAD_SIZE:].astype(jnp.bfloat16)
        group = lax.dynamic_slice_in_dim(key_value_pool, (shard * group_tokens).astype(jnp.int32), group_tokens, 0)
        live = prefix_mask(ids - (shard * GROUP_BLK).astype(jnp.int32), lens, GROUP_BLK, BLK)
        return attend(query_rows, key_new, value_new, group[:, :, :HEAD_SIZE], group[:, :, HEAD_SIZE:], live)

    shards = REQUEST_COUNT // SHARD_REQUESTS
    output_rows = lax.map(one_shard, (tokens.reshape(shards, SHARD_REQUESTS, MODEL_WIDTH), adapter_per_request.reshape(shards, SHARD_REQUESTS),
                                  prefix_length.reshape(shards, SHARD_REQUESTS), prefix_block_list.reshape(shards, SHARD_REQUESTS, MAXB),
                                  jnp.arange(shards, dtype=jnp.int32)))
    return output_rows.reshape(REQUEST_COUNT, KEY_VALUE_HEADS, QUERY_PER_KEY * HEAD_SIZE)
```

```python
import functools

import jax
import jax.numpy as jnp
from jax import lax
from jax.experimental import pallas as pl
from jax.experimental.pallas import tpu as pltpu
from jax.sharding import PartitionSpec as P

QUERY_PER_KEY = 8
HEAD_SIZE = 128
CAP = 16
BLK = 16
LANES = 128
DEPTH = 512
PARTS = (6, 4, 6)

ROPE_THETA = 500000.0
ADAPTER_SCALE = 2.0


def spread_columns(tok_ref, e_ref, z_ref):
    rows = tok_ref.shape[0]
    for c in range(tok_ref.shape[1] // LANES):
        wide = jnp.dot(
            tok_ref[:, c * LANES : (c + 1) * LANES], e_ref[...], preferred_element_type=jnp.float32
        ).astype(jnp.bfloat16)
        cols = slice(c * 2 * LANES, (c + 1) * 2 * LANES)
        z_ref[:rows, cols] = wide[:, : 2 * LANES]
        z_ref[rows:, cols] = wide[:, 2 * LANES :]


def projection_kernel(columns, has_base, *refs):
    tiles = columns // LANES
    tok_ref = refs[0]
    w_refs = refs[1 : 1 + tiles]
    base_ref = refs[1 + tiles] if has_base else None
    out_ref, e_ref, z_ref = refs[-3:]
    depth = tok_ref.shape[1]

    @pl.when(pl.program_id(0) == 0)
    def _():
        row = lax.broadcasted_iota(jnp.int32, (LANES, 4 * LANES), 0)
        col = lax.broadcasted_iota(jnp.int32, (LANES, 4 * LANES), 1)
        goal = jnp.where(col < 2 * LANES, 2 * row, 2 * row + 1 + 2 * LANES)
        e_ref[...] = (col == goal).astype(jnp.float32).astype(jnp.bfloat16)
        if has_base:
            out_ref[...] = base_ref[...]
        else:
            out_ref[...] = jnp.zeros_like(out_ref)

    spread_columns(tok_ref, e_ref, z_ref)
    for j in range(0, tiles, 2):
        pair = [w_refs[i].reshape(2 * depth, LANES)[...] for i in range(j, min(j + 2, tiles))]
        weight = jnp.concatenate(pair, axis=1) if len(pair) > 1 else pair[0]
        cols = slice(j * LANES, j * LANES + weight.shape[1])
        out_ref[:, cols] += jnp.dot(z_ref[...], weight, preferred_element_type=jnp.float32)


def projection_part(tokens, joined_weight, base, first, steps):
    rows = tokens.shape[0]
    columns = joined_weight.shape[2]
    tiles = columns // LANES
    in_specs = [pl.BlockSpec((rows, DEPTH), lambda k: (0, k + first))]
    for c in range(tiles):
        in_specs.append(
            pl.BlockSpec((DEPTH, 2, LANES), functools.partial(lambda c, k: (k + first, 0, c), c))
        )
    operands = [tokens] + [joined_weight] * tiles
    if base is not None:
        in_specs.append(pl.BlockSpec((2 * rows, columns), lambda k: (0, 0)))
        operands.append(base)
    return pl.pallas_call(
        functools.partial(projection_kernel, columns, base is not None),
        grid=(steps,),
        in_specs=in_specs,
        out_specs=pl.BlockSpec((2 * rows, columns), lambda k: (0, 0)),
        out_shape=jax.ShapeDtypeStruct((2 * rows, columns), jnp.float32),
        scratch_shapes=[
            pltpu.VMEM((LANES, 4 * LANES), jnp.bfloat16),
            pltpu.VMEM((2 * rows, 2 * DEPTH), jnp.bfloat16),
        ],
        compiler_params=pltpu.CompilerParams(vmem_limit_bytes=32 << 20),
        cost_estimate=pl.CostEstimate(
            flops=8 * rows * DEPTH * steps * columns,
            bytes_accessed=4 * DEPTH * steps * columns,
            transcendentals=0,
        ),
        name="projection",
    )(*operands)


def plain_projection(tokens, joined_weight):
    rows, width = tokens.shape
    heads, columns = joined_weight.shape[1:]
    if heads == 2:
        total = width // DEPTH
        parts = PARTS if sum(PARTS) == total else (total,)
        first, base = 0, None
        for steps in parts:
            base = projection_part(tokens, joined_weight, base, first, steps)
            first += steps
        return base
    out = jnp.dot(
        tokens, joined_weight.reshape(width, heads * columns), preferred_element_type=jnp.float32
    )
    return jnp.transpose(out.reshape(rows, heads, columns), (1, 0, 2)).reshape(heads * rows, columns)


def attention_kernel(plain_ref, back_ref, dest_ref, len_ref, ids_ref, cos_ref, sin_ref, pool_ref, out_ref):
    heads, rows, _ = out_ref.shape
    slots = back_ref.shape[0] * back_ref.shape[2]
    count = pool_ref.shape[0] * pool_ref.shape[2]
    scale = 1.0 / HEAD_SIZE**0.5
    pick = (lax.broadcasted_iota(jnp.int32, (rows, slots), 1) == dest_ref[...]).astype(
        jnp.float32
    ).astype(jnp.bfloat16)
    token = lax.broadcasted_iota(jnp.int32, (rows, count), 1)
    block, offset = token // BLK, token % BLK
    lens = len_ref[...]
    live = jnp.zeros((rows, count), jnp.float32)
    for j in range(ids_ref.shape[1]):
        hit = (ids_ref[:, j : j + 1] == block) & (offset + j * BLK < lens)
        live = jnp.where(hit, 1.0, live)
    cosine, sine = cos_ref[...], sin_ref[...]

    def rope(v):
        return (v * cosine + pltpu.roll(v, HEAD_SIZE // 2, 1) * sine).astype(jnp.bfloat16)

    for h in range(heads):
        update = jnp.dot(
            pick, back_ref[:, h].reshape(slots, back_ref.shape[3]), preferred_element_type=jnp.float32
        )
        joined = plain_ref[h * rows : (h + 1) * rows, :] + ADAPTER_SCALE * update
        key_new = rope(joined[:, QUERY_PER_KEY * HEAD_SIZE : (QUERY_PER_KEY + 1) * HEAD_SIZE])
        key_new = key_new.astype(jnp.float32)
        value_new = joined[:, (QUERY_PER_KEY + 1) * HEAD_SIZE :].astype(jnp.bfloat16)
        value_new = value_new.astype(jnp.float32)
        keys = pool_ref[:, h, :, :HEAD_SIZE].reshape(count, HEAD_SIZE)
        value_rows = pool_ref[:, h, :, HEAD_SIZE:].reshape(count, HEAD_SIZE)
        for g in range(QUERY_PER_KEY):
            query = rope(joined[:, g * HEAD_SIZE : (g + 1) * HEAD_SIZE])
            scores = (
                lax.dot_general(
                    query, keys, (((1,), (1,)), ((), ())), preferred_element_type=jnp.float32
                )
                * scale
            )
            own = jnp.sum(query.astype(jnp.float32) * key_new, axis=1, keepdims=True) * scale
            scores = jnp.where(live > 0.0, scores, -jnp.inf)
            top = jnp.maximum(jnp.max(scores, axis=1, keepdims=True), own)
            prob = jnp.exp(scores - top)
            prob_own = jnp.exp(own - top)
            total = jnp.sum(prob, axis=1, keepdims=True) + prob_own
            mixed = jnp.dot(prob.astype(jnp.bfloat16), value_rows, preferred_element_type=jnp.float32)
            mixed = mixed + prob_own.astype(jnp.bfloat16).astype(jnp.float32) * value_new
            out_ref[h, :, g * HEAD_SIZE : (g + 1) * HEAD_SIZE] = (mixed / total).astype(jnp.bfloat16)


def attention(plain, back, dest, lens, ids, cosine, sine, pool, rows, heads):
    return pl.pallas_call(
        attention_kernel,
        out_shape=jax.ShapeDtypeStruct((heads, rows, QUERY_PER_KEY * HEAD_SIZE), jnp.bfloat16),
        in_specs=[pl.BlockSpec(memory_space=pltpu.VMEM)] * 8,
        out_specs=pl.BlockSpec(memory_space=pltpu.VMEM),
        compiler_params=pltpu.CompilerParams(vmem_limit_bytes=24 << 20),
        name="attention",
    )(plain, back, dest, lens, ids, cosine, sine, pool)


def routing(adapter_per_request, adapter_store_slot, shards, request_shard, shard_adapters, shard):
    adapters = adapter_store_slot.shape[0]
    match = adapter_per_request[:, None] == jnp.arange(adapters, dtype=jnp.int32)[None, :]
    store_slot = jnp.sum(jnp.where(match, adapter_store_slot[None, :], 0), axis=1).reshape(
        shards, request_shard
    )
    owner = store_slot // shard_adapters
    local = store_slot - owner * shard_adapters
    index = jnp.arange(request_shard, dtype=jnp.int32)
    earlier = index[:, None] < index[None, :]
    same = owner[:, :, None] == owner[:, None, :]
    rank = jnp.sum((same & earlier[None]).astype(jnp.int32), axis=1)
    owner_mine = lax.dynamic_index_in_dim(owner, shard, 0, keepdims=False)
    rank_mine = lax.dynamic_index_in_dim(rank, shard, 0, keepdims=False)
    dest = owner_mine * CAP + rank_mine
    place = jnp.where(owner == shard, rank, -1)
    chosen = place[:, None, :] == jnp.arange(CAP, dtype=jnp.int32)[None, :, None]
    arrived = jnp.sum(jnp.where(chosen, local[:, None, :] + 1, 0), axis=2) - 1
    return dest, arrived


def body(
    tokens,
    joined_weight,
    down_weight,
    up_weight,
    adapter_per_request,
    adapter_store_slot,
    prefix_block_list,
    prefix_length,
    key_value_pool,
):
    n_store = lax.axis_size("store")
    n_ctx = lax.axis_size("ctx")
    shard = lax.axis_index("store")
    member = lax.axis_index("ctx")
    request_shard = tokens.shape[0]
    shard_adapters, width_slice, rank_size = down_weight.shape
    head_slice = joined_weight.shape[1]
    columns = joined_weight.shape[2]
    pool_rows = key_value_pool.shape[0]

    dest, arrived = routing(
        adapter_per_request, adapter_store_slot, n_store, request_shard, shard_adapters, shard
    )
    slots = n_store * CAP
    x_local = lax.dynamic_slice_in_dim(tokens, member * width_slice, width_slice, 1)
    place = (jnp.arange(slots, dtype=jnp.int32)[:, None] == dest[None, :]).astype(jnp.bfloat16)
    outgoing = jnp.dot(place, x_local, preferred_element_type=jnp.float32).astype(jnp.bfloat16)
    received = lax.all_to_all(
        outgoing.reshape(n_store, CAP, width_slice), "store", split_axis=0, concat_axis=0, tiled=True
    )
    pool = jnp.transpose(key_value_pool, (1, 0, 2)).reshape(
        n_ctx, head_slice, pool_rows, 2 * HEAD_SIZE
    )
    pool = lax.all_to_all(pool, "ctx", split_axis=0, concat_axis=0, tiled=True)

    hot = arrived[:, :, None] == jnp.arange(shard_adapters, dtype=jnp.int32)[None, None, :]
    value_partial = jnp.einsum(
        "hbm,gmq->hbgq", received, down_weight, preferred_element_type=jnp.float32
    )
    shrunk_part = jnp.sum(jnp.where(hot[..., None], value_partial, 0.0), axis=2)
    copies = jnp.broadcast_to(shrunk_part[None], (n_ctx,) + shrunk_part.shape)
    partials = lax.all_to_all(copies, "ctx", split_axis=0, concat_axis=0, tiled=True)
    shrunk = jnp.sum(partials, axis=0).astype(jnp.bfloat16)
    spread_rows = jnp.where(hot[..., None], shrunk[:, :, None, :], jnp.zeros((), jnp.bfloat16))
    update = jnp.einsum(
        "oxbl,blpj->opxj", spread_rows, up_weight, preferred_element_type=jnp.float32
    ).astype(jnp.bfloat16)
    back = lax.all_to_all(update, "store", split_axis=0, concat_axis=0, tiled=True)

    plain = plain_projection(tokens, joined_weight)

    half = HEAD_SIZE // 2
    freq = jnp.power(ROPE_THETA, -(jnp.arange(half, dtype=jnp.float32) * 2.0 / HEAD_SIZE))
    angle = prefix_length.astype(jnp.float32)[:, None] * freq
    cosine, sine = jnp.cos(angle), jnp.sin(angle)
    group_blocks = pool_rows * n_ctx // BLK
    out = attention(
        plain,
        back,
        dest[:, None],
        prefix_length[:, None],
        prefix_block_list - shard * group_blocks,
        jnp.concatenate([cosine, cosine], axis=1),
        jnp.concatenate([-sine, sine], axis=1),
        pool,
        request_shard,
        head_slice,
    )
    return jnp.transpose(out, (1, 0, 2))


def solution(mesh):
    in_specs = (
        P("store", None),
        P(None, "ctx", None),
        P("store", "ctx", None),
        P("store", None, "ctx", None),
        P(),
        P(),
        P("store", None),
        P("store"),
        P(("store", "ctx"), None, None),
    )
    out_specs = P("store", "ctx", None)
    return jax.shard_map(body, mesh=mesh, in_specs=in_specs, out_specs=out_specs, check_vma=False)
```

```python
import functools

import jax
import jax.numpy as jnp
from jax import lax
from jax.experimental import pallas as pl
from jax.experimental.pallas import tpu as pltpu
from jax.sharding import PartitionSpec as P

QUERY_PER_KEY = 8
HEAD_SIZE = 128
CAP = 16
BLK = 16
LANES = 128
DEPTH = 512
PARTS = (6, 4, 6)

ROPE_THETA = 500000.0
ADAPTER_SCALE = 2.0


def spread_columns(tok_ref, e_ref, z_ref):
    rows = tok_ref.shape[0]
    for c in range(tok_ref.shape[1] // LANES):
        wide = jnp.dot(
            tok_ref[:, c * LANES : (c + 1) * LANES], e_ref[...], preferred_element_type=jnp.float32
        ).astype(jnp.bfloat16)
        cols = slice(c * 2 * LANES, (c + 1) * 2 * LANES)
        z_ref[:rows, cols] = wide[:, : 2 * LANES]
        z_ref[rows:, cols] = wide[:, 2 * LANES :]


def projection_kernel(columns, has_base, *refs):
    tiles = columns // LANES
    tok_ref = refs[0]
    w_refs = refs[1 : 1 + tiles]
    base_ref = refs[1 + tiles] if has_base else None
    out_ref, e_ref, z_ref = refs[-3:]
    depth = tok_ref.shape[1]

    @pl.when(pl.program_id(0) == 0)
    def _():
        row = lax.broadcasted_iota(jnp.int32, (LANES, 4 * LANES), 0)
        col = lax.broadcasted_iota(jnp.int32, (LANES, 4 * LANES), 1)
        goal = jnp.where(col < 2 * LANES, 2 * row, 2 * row + 1 + 2 * LANES)
        e_ref[...] = (col == goal).astype(jnp.float32).astype(jnp.bfloat16)
        if has_base:
            out_ref[...] = base_ref[...]
        else:
            out_ref[...] = jnp.zeros_like(out_ref)

    spread_columns(tok_ref, e_ref, z_ref)
    for j in range(0, tiles, 2):
        pair = [w_refs[i].reshape(2 * depth, LANES)[...] for i in range(j, min(j + 2, tiles))]
        weight = jnp.concatenate(pair, axis=1) if len(pair) > 1 else pair[0]
        cols = slice(j * LANES, j * LANES + weight.shape[1])
        out_ref[:, cols] += jnp.dot(z_ref[...], weight, preferred_element_type=jnp.float32)


def projection_part(tokens, joined_weight, base, first, steps):
    rows = tokens.shape[0]
    columns = joined_weight.shape[2]
    tiles = columns // LANES
    in_specs = [pl.BlockSpec((rows, DEPTH), lambda k: (0, k + first))]
    for c in range(tiles):
        in_specs.append(
            pl.BlockSpec((DEPTH, 2, LANES), functools.partial(lambda c, k: (k + first, 0, c), c))
        )
    operands = [tokens] + [joined_weight] * tiles
    if base is not None:
        in_specs.append(pl.BlockSpec((2 * rows, columns), lambda k: (0, 0)))
        operands.append(base)
    return pl.pallas_call(
        functools.partial(projection_kernel, columns, base is not None),
        grid=(steps,),
        in_specs=in_specs,
        out_specs=pl.BlockSpec((2 * rows, columns), lambda k: (0, 0)),
        out_shape=jax.ShapeDtypeStruct((2 * rows, columns), jnp.float32),
        scratch_shapes=[
            pltpu.VMEM((LANES, 4 * LANES), jnp.bfloat16),
            pltpu.VMEM((2 * rows, 2 * DEPTH), jnp.bfloat16),
        ],
        compiler_params=pltpu.CompilerParams(vmem_limit_bytes=32 << 20),
        cost_estimate=pl.CostEstimate(
            flops=8 * rows * DEPTH * steps * columns,
            bytes_accessed=4 * DEPTH * steps * columns,
            transcendentals=0,
        ),
        name="projection",
    )(*operands)


def plain_projection(tokens, joined_weight):
    rows, width = tokens.shape
    heads, columns = joined_weight.shape[1:]
    if heads == 2:
        total = width // DEPTH
        parts = PARTS if sum(PARTS) == total else (total,)
        first, base = 0, None
        for steps in parts:
            base = projection_part(tokens, joined_weight, base, first, steps)
            first += steps
        return base
    out = jnp.dot(
        tokens, joined_weight.reshape(width, heads * columns), preferred_element_type=jnp.float32
    )
    return jnp.transpose(out.reshape(rows, heads, columns), (1, 0, 2)).reshape(heads * rows, columns)


def attention_kernel(plain_ref, back_ref, dest_ref, len_ref, ids_ref, cos_ref, sin_ref, pool_ref, out_ref):
    heads, rows, _ = out_ref.shape
    slots = back_ref.shape[0] * back_ref.shape[2]
    count = pool_ref.shape[0] * pool_ref.shape[2]
    scale = 1.0 / HEAD_SIZE**0.5
    pick = (lax.broadcasted_iota(jnp.int32, (rows, slots), 1) == dest_ref[...]).astype(
        jnp.float32
    ).astype(jnp.bfloat16)
    token = lax.broadcasted_iota(jnp.int32, (rows, count), 1)
    block, offset = token // BLK, token % BLK
    lens = len_ref[...]
    live = jnp.zeros((rows, count), jnp.float32)
    for j in range(ids_ref.shape[1]):
        hit = (ids_ref[:, j : j + 1] == block) & (offset + j * BLK < lens)
        live = jnp.where(hit, 1.0, live)
    cosine, sine = cos_ref[...], sin_ref[...]

    def rope(v):
        return (v * cosine + pltpu.roll(v, HEAD_SIZE // 2, 1) * sine).astype(jnp.bfloat16)

    for h in range(heads):
        update = jnp.dot(
            pick, back_ref[:, h].reshape(slots, back_ref.shape[3]), preferred_element_type=jnp.float32
        )
        joined = plain_ref[h * rows : (h + 1) * rows, :] + ADAPTER_SCALE * update
        key_new = rope(joined[:, QUERY_PER_KEY * HEAD_SIZE : (QUERY_PER_KEY + 1) * HEAD_SIZE])
        key_new = key_new.astype(jnp.float32)
        value_new = joined[:, (QUERY_PER_KEY + 1) * HEAD_SIZE :].astype(jnp.bfloat16)
        value_new = value_new.astype(jnp.float32)
        keys = pool_ref[:, h, :, :HEAD_SIZE].reshape(count, HEAD_SIZE)
        value_rows = pool_ref[:, h, :, HEAD_SIZE:].reshape(count, HEAD_SIZE)
        for g in range(QUERY_PER_KEY):
            query = rope(joined[:, g * HEAD_SIZE : (g + 1) * HEAD_SIZE])
            scores = (
                lax.dot_general(
                    query, keys, (((1,), (1,)), ((), ())), preferred_element_type=jnp.float32
                )
                * scale
            )
            own = jnp.sum(query.astype(jnp.float32) * key_new, axis=1, keepdims=True) * scale
            scores = jnp.where(live > 0.0, scores, -jnp.inf)
            top = jnp.maximum(jnp.max(scores, axis=1, keepdims=True), own)
            prob = jnp.exp(scores - top)
            prob_own = jnp.exp(own - top)
            total = jnp.sum(prob, axis=1, keepdims=True) + prob_own
            mixed = jnp.dot(prob.astype(jnp.bfloat16), value_rows, preferred_element_type=jnp.float32)
            mixed = mixed + prob_own.astype(jnp.bfloat16).astype(jnp.float32) * value_new
            out_ref[h, :, g * HEAD_SIZE : (g + 1) * HEAD_SIZE] = (mixed / total).astype(jnp.bfloat16)


def attention(plain, back, dest, lens, ids, cosine, sine, pool, rows, heads):
    return pl.pallas_call(
        attention_kernel,
        out_shape=jax.ShapeDtypeStruct((heads, rows, QUERY_PER_KEY * HEAD_SIZE), jnp.bfloat16),
        in_specs=[pl.BlockSpec(memory_space=pltpu.VMEM)] * 8,
        out_specs=pl.BlockSpec(memory_space=pltpu.VMEM),
        compiler_params=pltpu.CompilerParams(vmem_limit_bytes=24 << 20),
        name="attention",
    )(plain, back, dest, lens, ids, cosine, sine, pool)


MESH = pl.DeviceIdType.MESH
DOWN_STEP = 5
UP_STEP = 9


def attend_rows(plain_ref, back_ref, pick, live, cosine, sine, pool_ref, out_ref):
    heads, rows, _ = out_ref.shape
    slots = back_ref.shape[0] * back_ref.shape[2]
    count = pool_ref.shape[0] * pool_ref.shape[2]
    scale = 1.0 / HEAD_SIZE**0.5

    def rope(v):
        return (v * cosine + pltpu.roll(v, HEAD_SIZE // 2, 1) * sine).astype(jnp.bfloat16)

    for h in range(heads):
        update = jnp.dot(
            pick, back_ref[:, h].reshape(slots, back_ref.shape[3]), preferred_element_type=jnp.float32
        )
        joined = plain_ref[h * rows : (h + 1) * rows, :] + ADAPTER_SCALE * update
        key_new = rope(joined[:, QUERY_PER_KEY * HEAD_SIZE : (QUERY_PER_KEY + 1) * HEAD_SIZE])
        key_new = key_new.astype(jnp.float32)
        value_new = joined[:, (QUERY_PER_KEY + 1) * HEAD_SIZE :].astype(jnp.bfloat16)
        value_new = value_new.astype(jnp.float32)
        keys = pool_ref[:, h, :, :HEAD_SIZE].reshape(count, HEAD_SIZE)
        value_rows = pool_ref[:, h, :, HEAD_SIZE:].reshape(count, HEAD_SIZE)
        for g in range(QUERY_PER_KEY):
            query = rope(joined[:, g * HEAD_SIZE : (g + 1) * HEAD_SIZE])
            scores = (
                lax.dot_general(
                    query, keys, (((1,), (1,)), ((), ())), preferred_element_type=jnp.float32
                )
                * scale
            )
            own = jnp.sum(query.astype(jnp.float32) * key_new, axis=1, keepdims=True) * scale
            scores = jnp.where(live > 0.0, scores, -jnp.inf)
            top = jnp.maximum(jnp.max(scores, axis=1, keepdims=True), own)
            prob = jnp.exp(scores - top)
            prob_own = jnp.exp(own - top)
            total = jnp.sum(prob, axis=1, keepdims=True) + prob_own
            mixed = jnp.dot(prob.astype(jnp.bfloat16), value_rows, preferred_element_type=jnp.float32)
            mixed = mixed + prob_own.astype(jnp.bfloat16).astype(jnp.float32) * value_new
            out_ref[h, :, g * HEAD_SIZE : (g + 1) * HEAD_SIZE] = (mixed / total).astype(jnp.bfloat16)


def step_kernel(n_store, n_ctx, shard_adapters, tiles, *refs):
    tok_ref = refs[0]
    w_refs = refs[1 : 1 + tiles]
    (tok_hbm, down_hbm, up_hbm, pool_hbm, adapter_ref, slot_ref, ids_ref, len_ref, freq_ref, out_ref) = refs[
        1 + tiles : 11 + tiles
    ]
    (e_ref, z_ref, plain, xl, down, up, out_s, recv_s, part, sb, bk, poolr, place_s, hot_s, live_s,
     cos_s, sin_s, in_sem, up_sem, s1, r1, s2, r2, s3, r3, s4, r4) = refs[11 + tiles :]
    step = pl.program_id(0)
    last = pl.num_programs(0) - 1
    me = lax.axis_index("store")
    member = lax.axis_index("ctx")
    rows = tok_ref.shape[0]
    depth = tok_ref.shape[1]
    slots = n_store * CAP
    wide = down.shape[0]
    width = xl.shape[1]

    def store_copy(src, dst, send, recv, d):
        target = lax.rem(me + d, n_store)
        source = lax.rem(me + n_store - d, n_store)
        go = pltpu.make_async_remote_copy(
            src_ref=src.at[target], dst_ref=dst.at[me], send_sem=send.at[d - 1],
            recv_sem=recv.at[d - 1], device_id={"store": target}, device_id_type=MESH)
        come = pltpu.make_async_remote_copy(
            src_ref=src.at[target], dst_ref=dst.at[source], send_sem=send.at[d - 1],
            recv_sem=recv.at[d - 1], device_id={"store": target}, device_id_type=MESH)
        return go, come

    def ctx_copy(src, dst, send, recv, d, by_target):
        target = lax.rem(member + d, n_ctx)
        source = lax.rem(member + n_ctx - d, n_ctx)
        origin = src.at[target] if by_target else src.at[member]
        go = pltpu.make_async_remote_copy(
            src_ref=origin, dst_ref=dst.at[member], send_sem=send.at[d - 1],
            recv_sem=recv.at[d - 1], device_id={"ctx": target}, device_id_type=MESH)
        come = pltpu.make_async_remote_copy(
            src_ref=origin, dst_ref=dst.at[source], send_sem=send.at[d - 1],
            recv_sem=recv.at[d - 1], device_id={"ctx": target}, device_id_type=MESH)
        return go, come

    def local_copies():
        start = pl.multiple_of(member * width, width)
        first = pltpu.make_async_copy(tok_hbm.at[:, pl.ds(start, width)], xl, in_sem.at[0])
        second = pltpu.make_async_copy(down_hbm, down, in_sem.at[1])
        third = pltpu.make_async_copy(pool_hbm.at[member], poolr.at[member], in_sem.at[2])
        rest = [
            pltpu.make_async_copy(up_hbm.at[:, :, pl.ds(c * LANES, LANES)], up.at[c], up_sem.at[c])
            for c in range(tiles)
        ]
        return first, second, third, rest

    @pl.when(step == 0)
    def _():
        barrier = pltpu.get_barrier_semaphore()
        for d in range(1, n_store):
            pl.semaphore_signal(barrier, inc=1, device_id={"store": lax.rem(me + d, n_store)}, device_id_type=MESH)
        for d in range(1, n_ctx):
            pl.semaphore_signal(barrier, inc=1, device_id={"ctx": lax.rem(member + d, n_ctx)}, device_id_type=MESH)
        first, second, third, rest = local_copies()
        first.start()
        second.start()
        third.start()
        for copy in rest:
            copy.start()
        row = lax.broadcasted_iota(jnp.int32, (LANES, 4 * LANES), 0)
        col = lax.broadcasted_iota(jnp.int32, (LANES, 4 * LANES), 1)
        goal = jnp.where(col < 2 * LANES, 2 * row, 2 * row + 1 + 2 * LANES)
        e_ref[...] = (col == goal).astype(jnp.float32).astype(jnp.bfloat16)
        plain[...] = jnp.zeros_like(plain)

        adapters = adapter_ref[...]
        chosen = jnp.zeros_like(adapters)
        for a in range(slot_ref.shape[0]):
            chosen = jnp.where(adapters == a, slot_ref[a], chosen)
        owner = chosen // shard_adapters
        local = (chosen - owner * shard_adapters).astype(jnp.float32)
        before = lax.broadcasted_iota(jnp.int32, (rows, rows), 0)
        after = lax.broadcasted_iota(jnp.int32, (rows, rows), 1)
        earlier = (before < after).astype(jnp.float32).astype(jnp.bfloat16)
        rank = jnp.zeros(owner.shape, jnp.float32)
        for w in range(n_store):
            mine = (owner == w).astype(jnp.float32)
            counted = jnp.dot(mine.astype(jnp.bfloat16), earlier, preferred_element_type=jnp.float32)
            rank = rank + mine * counted
        dest = owner.astype(jnp.float32) * CAP + rank
        which = lax.broadcasted_iota(jnp.int32, owner.shape, 0)
        dest_mine = jnp.sum(jnp.where(which == me, dest, 0.0), axis=0, keepdims=True)
        slot_id = lax.broadcasted_iota(jnp.int32, (slots, rows), 0).astype(jnp.float32)
        place = (slot_id == dest_mine).astype(jnp.float32)
        place_s[...] = place
        here = jnp.where(owner == me, rank, -1.0)
        cap_id = lax.broadcasted_iota(jnp.int32, (CAP, rows), 0).astype(jnp.float32)
        arrived = jnp.concatenate(
            [
                jnp.sum(jnp.where(cap_id == here[o : o + 1, :], local[o : o + 1, :] + 1.0, 0.0), axis=1, keepdims=True)
                for o in range(n_store)
            ],
            axis=0,
        )
        adapter_id = (lax.broadcasted_iota(jnp.int32, (slots, wide), 1) // (wide // shard_adapters)).astype(jnp.float32)
        hot_s[...] = (adapter_id + 1.0 == arrived).astype(jnp.float32)

        first.wait()
        out_s[...] = jnp.dot(
            place.astype(jnp.bfloat16), xl[...], preferred_element_type=jnp.float32
        ).astype(jnp.bfloat16).reshape(n_store, CAP, width)
        recv_s[pl.ds(me, 1)] = out_s[pl.ds(me, 1)]
        pl.semaphore_wait(barrier, n_store + n_ctx - 2)
        for d in range(1, n_store):
            store_copy(out_s, recv_s, s1, r1, d)[0].start()
        for d in range(1, n_ctx):
            ctx_copy(pool_hbm, poolr, s4, r4, d, True)[0].start()

    @pl.when(step == 1)
    def _():
        count = live_s.shape[1]
        token = lax.broadcasted_iota(jnp.int32, (count, rows), 0)
        block, offset = token // BLK, token % BLK
        live = jnp.zeros((count, rows), jnp.float32)
        for j in range(ids_ref.shape[0]):
            hit = (ids_ref[j : j + 1, :] - me * (count // BLK) == block) & (offset + j * BLK < len_ref[...])
            live = jnp.where(hit, 1.0, live)
        live_s[...] = live.T
        lens = jnp.broadcast_to(len_ref[...].astype(jnp.float32), (rows, rows)).T
        angle = lens * freq_ref[...]
        cos_s[...] = jnp.cos(angle)
        lane = lax.broadcasted_iota(jnp.int32, (rows, HEAD_SIZE), 1)
        sine = jnp.sin(angle)
        sin_s[...] = jnp.where(lane < HEAD_SIZE // 2, -sine, sine)

    @pl.when(step == DOWN_STEP)
    def _():
        for d in range(1, n_store):
            go, come = store_copy(out_s, recv_s, s1, r1, d)
            go.wait_send()
            come.wait_recv()
        local_copies()[1].wait()
        value = lax.dot_general(
            recv_s[...].reshape(slots, width), down[...], (((1,), (1,)), ((), ())),
            preferred_element_type=jnp.float32)
        value = jnp.where(hot_s[...] > 0.0, value, 0.0)
        folded = value[:, :LANES]
        for c in range(1, wide // LANES):
            folded = folded + value[:, c * LANES : (c + 1) * LANES]
        part[member] = folded
        for d in range(1, n_ctx):
            ctx_copy(part, part, s2, r2, d, False)[0].start()

    @pl.when(step == UP_STEP)
    def _():
        for d in range(1, n_ctx):
            go, come = ctx_copy(part, part, s2, r2, d, False)
            go.wait_send()
            come.wait_recv()
        for copy in local_copies()[3]:
            copy.wait()
        total = part[0]
        for c in range(1, n_ctx):
            total = total + part[c]
        total = (total + pltpu.roll(total, LANES // 2, 1)).astype(jnp.bfloat16).astype(jnp.float32)
        for c in range(wide // LANES):
            cols = slice(c * LANES, (c + 1) * LANES)
            spread = (total * hot_s[:, cols]).astype(jnp.bfloat16)
            pair = jnp.dot(spread, e_ref[...], preferred_element_type=jnp.float32).astype(jnp.bfloat16)
            z_ref[:slots, 2 * c * LANES : 2 * (c + 1) * LANES] = pair[:, : 2 * LANES]
            z_ref[slots:, 2 * c * LANES : 2 * (c + 1) * LANES] = pair[:, 2 * LANES :]
        for j in range(0, tiles, 2):
            weight = jnp.concatenate(
                [up.at[i].reshape(2 * wide, LANES)[...] for i in (j, j + 1)], axis=1)
            update = jnp.dot(z_ref[:, : 2 * wide], weight, preferred_element_type=jnp.float32).astype(jnp.bfloat16)
            cols = slice(j * LANES, (j + 2) * LANES)
            for h in range(2):
                sb[:, h, :, cols] = update[h * slots : (h + 1) * slots].reshape(n_store, CAP, 2 * LANES)
        bk[pl.ds(me, 1)] = sb[pl.ds(me, 1)]
        for d in range(1, n_store):
            store_copy(sb, bk, s3, r3, d)[0].start()

    spread_columns(tok_ref, e_ref, z_ref)
    for j in range(0, tiles, 2):
        weight = jnp.concatenate(
            [w_refs[i].reshape(2 * depth, LANES)[...] for i in (j, j + 1)], axis=1)
        cols = slice(j * LANES, (j + 2) * LANES)
        plain[:, cols] += jnp.dot(z_ref[...], weight, preferred_element_type=jnp.float32)

    @pl.when(step == last)
    def _():
        local_copies()[2].wait()
        for d in range(1, n_ctx):
            go, come = ctx_copy(pool_hbm, poolr, s4, r4, d, True)
            go.wait_send()
            come.wait_recv()
        for d in range(1, n_store):
            go, come = store_copy(sb, bk, s3, r3, d)
            go.wait_send()
            come.wait_recv()
        pick = place_s[...].T.astype(jnp.bfloat16)
        attend_rows(plain, bk, pick, live_s[...], cos_s[...], sin_s[...], poolr, out_ref)


def fused(tokens, joined_weight, down_weight, up_weight, adapter_per_request, adapter_store_slot,
          prefix_block_list, prefix_length, key_value_pool):
    n_store = lax.axis_size("store")
    n_ctx = lax.axis_size("ctx")
    rows, d_model = tokens.shape
    shard_adapters, width, rank_size = down_weight.shape
    heads, columns = joined_weight.shape[1:]
    tiles = columns // LANES
    pool_rows = key_value_pool.shape[0]
    slots = n_store * CAP
    wide = shard_adapters * rank_size
    bf, f32 = jnp.bfloat16, jnp.float32
    down = jnp.transpose(down_weight, (0, 2, 1)).reshape(wide, width)
    up = up_weight.reshape(wide, heads, columns)
    pool = jnp.transpose(key_value_pool, (1, 0, 2)).reshape(n_ctx, heads, pool_rows, 2 * HEAD_SIZE)
    half = HEAD_SIZE // 2
    freq = jnp.power(ROPE_THETA, -(jnp.arange(half, dtype=f32) * 2.0 / HEAD_SIZE))
    freq = jnp.concatenate([freq, freq])[None]
    hbm = pl.BlockSpec(memory_space=pl.ANY)

    def whole_block(shape):
        return pl.BlockSpec(shape, lambda k: (0, 0))

    in_specs = [pl.BlockSpec((rows, DEPTH), lambda k: (0, k))]
    for c in range(tiles):
        in_specs.append(pl.BlockSpec((DEPTH, 2, LANES), functools.partial(lambda c, k: (k, 0, c), c)))
    in_specs += [hbm] * 4 + [
        whole_block((n_store, rows)),
        pl.BlockSpec(memory_space=pltpu.SMEM),
        whole_block(prefix_block_list.shape[::-1]),
        whole_block((1, rows)),
        whole_block((1, HEAD_SIZE)),
    ]
    dma = pltpu.SemaphoreType.DMA
    out = pl.pallas_call(
        functools.partial(step_kernel, n_store, n_ctx, shard_adapters, tiles),
        grid=(d_model // DEPTH,),
        in_specs=in_specs,
        out_specs=pl.BlockSpec((heads, rows, QUERY_PER_KEY * HEAD_SIZE), lambda k: (0, 0, 0)),
        out_shape=jax.ShapeDtypeStruct((heads, rows, QUERY_PER_KEY * HEAD_SIZE), bf),
        scratch_shapes=[
            pltpu.VMEM((LANES, 4 * LANES), bf),
            pltpu.VMEM((2 * rows, 2 * DEPTH), bf),
            pltpu.VMEM((2 * rows, columns), f32),
            pltpu.VMEM((rows, width), bf),
            pltpu.VMEM((wide, width), bf),
            pltpu.VMEM((tiles, wide, 2, LANES), bf),
            pltpu.VMEM((n_store, CAP, width), bf),
            pltpu.VMEM((n_store, CAP, width), bf),
            pltpu.VMEM((n_ctx, slots, LANES), f32),
            pltpu.VMEM((n_store, heads, CAP, columns), bf),
            pltpu.VMEM((n_store, heads, CAP, columns), bf),
            pltpu.VMEM((n_ctx, heads, pool_rows, 2 * HEAD_SIZE), bf),
            pltpu.VMEM((slots, rows), f32),
            pltpu.VMEM((slots, wide), f32),
            pltpu.VMEM((rows, n_ctx * pool_rows), f32),
            pltpu.VMEM((rows, HEAD_SIZE), f32),
            pltpu.VMEM((rows, HEAD_SIZE), f32),
            dma((3,)),
            dma((tiles,)),
            dma((n_store - 1,)),
            dma((n_store - 1,)),
            dma((n_ctx - 1,)),
            dma((n_ctx - 1,)),
            dma((n_store - 1,)),
            dma((n_store - 1,)),
            dma((n_ctx - 1,)),
            dma((n_ctx - 1,)),
        ],
        compiler_params=pltpu.CompilerParams(
            vmem_limit_bytes=48 << 20, collective_id=0, has_side_effects=True
        ),
        name="decode_step",
    )(
        tokens, *([joined_weight] * tiles), tokens, down, up, pool,
        adapter_per_request.reshape(n_store, rows), adapter_store_slot, prefix_block_list.T,
        prefix_length[None], freq,
    )
    return jnp.transpose(out, (1, 0, 2))


def routing(adapter_per_request, adapter_store_slot, shards, request_shard, shard_adapters, shard):
    adapters = adapter_store_slot.shape[0]
    match = adapter_per_request[:, None] == jnp.arange(adapters, dtype=jnp.int32)[None, :]
    store_slot = jnp.sum(jnp.where(match, adapter_store_slot[None, :], 0), axis=1).reshape(
        shards, request_shard
    )
    owner = store_slot // shard_adapters
    local = store_slot - owner * shard_adapters
    index = jnp.arange(request_shard, dtype=jnp.int32)
    earlier = index[:, None] < index[None, :]
    same = owner[:, :, None] == owner[:, None, :]
    rank = jnp.sum((same & earlier[None]).astype(jnp.int32), axis=1)
    owner_mine = lax.dynamic_index_in_dim(owner, shard, 0, keepdims=False)
    rank_mine = lax.dynamic_index_in_dim(rank, shard, 0, keepdims=False)
    dest = owner_mine * CAP + rank_mine
    place = jnp.where(owner == shard, rank, -1)
    chosen = place[:, None, :] == jnp.arange(CAP, dtype=jnp.int32)[None, :, None]
    arrived = jnp.sum(jnp.where(chosen, local[:, None, :] + 1, 0), axis=2) - 1
    return dest, arrived


def body(
    tokens,
    joined_weight,
    down_weight,
    up_weight,
    adapter_per_request,
    adapter_store_slot,
    prefix_block_list,
    prefix_length,
    key_value_pool,
):
    n_store = lax.axis_size("store")
    n_ctx = lax.axis_size("ctx")
    shard = lax.axis_index("store")
    member = lax.axis_index("ctx")
    request_shard = tokens.shape[0]
    shard_adapters, width_slice, rank_size = down_weight.shape
    head_slice = joined_weight.shape[1]
    columns = joined_weight.shape[2]
    slots = n_store * CAP
    if (
        head_slice == 2
        and slots == request_shard
        and tokens.shape[1] % DEPTH == 0
        and tokens.shape[1] // DEPTH > UP_STEP + 1
        and shard_adapters * rank_size <= DEPTH
        and rank_size * 2 == LANES
        and columns % (2 * LANES) == 0
    ):
        return fused(
            tokens, joined_weight, down_weight, up_weight, adapter_per_request, adapter_store_slot,
            prefix_block_list, prefix_length, key_value_pool,
        )
    pool_rows = key_value_pool.shape[0]

    dest, arrived = routing(
        adapter_per_request, adapter_store_slot, n_store, request_shard, shard_adapters, shard
    )
    slots = n_store * CAP
    x_local = lax.dynamic_slice_in_dim(tokens, member * width_slice, width_slice, 1)
    place = (jnp.arange(slots, dtype=jnp.int32)[:, None] == dest[None, :]).astype(jnp.bfloat16)
    outgoing = jnp.dot(place, x_local, preferred_element_type=jnp.float32).astype(jnp.bfloat16)
    received = lax.all_to_all(
        outgoing.reshape(n_store, CAP, width_slice), "store", split_axis=0, concat_axis=0, tiled=True
    )
    pool = jnp.transpose(key_value_pool, (1, 0, 2)).reshape(
        n_ctx, head_slice, pool_rows, 2 * HEAD_SIZE
    )
    pool = lax.all_to_all(pool, "ctx", split_axis=0, concat_axis=0, tiled=True)

    hot = arrived[:, :, None] == jnp.arange(shard_adapters, dtype=jnp.int32)[None, None, :]
    value_partial = jnp.einsum(
        "hbm,gmq->hbgq", received, down_weight, preferred_element_type=jnp.float32
    )
    shrunk_part = jnp.sum(jnp.where(hot[..., None], value_partial, 0.0), axis=2)
    copies = jnp.broadcast_to(shrunk_part[None], (n_ctx,) + shrunk_part.shape)
    partials = lax.all_to_all(copies, "ctx", split_axis=0, concat_axis=0, tiled=True)
    shrunk = jnp.sum(partials, axis=0).astype(jnp.bfloat16)
    spread_rows = jnp.where(hot[..., None], shrunk[:, :, None, :], jnp.zeros((), jnp.bfloat16))
    update = jnp.einsum(
        "oxbl,blpj->opxj", spread_rows, up_weight, preferred_element_type=jnp.float32
    ).astype(jnp.bfloat16)
    back = lax.all_to_all(update, "store", split_axis=0, concat_axis=0, tiled=True)

    plain = plain_projection(tokens, joined_weight)

    half = HEAD_SIZE // 2
    freq = jnp.power(ROPE_THETA, -(jnp.arange(half, dtype=jnp.float32) * 2.0 / HEAD_SIZE))
    angle = prefix_length.astype(jnp.float32)[:, None] * freq
    cosine, sine = jnp.cos(angle), jnp.sin(angle)
    group_blocks = pool_rows * n_ctx // BLK
    out = attention(
        plain,
        back,
        dest[:, None],
        prefix_length[:, None],
        prefix_block_list - shard * group_blocks,
        jnp.concatenate([cosine, cosine], axis=1),
        jnp.concatenate([-sine, sine], axis=1),
        pool,
        request_shard,
        head_slice,
    )
    return jnp.transpose(out, (1, 0, 2))


def solution(mesh):
    in_specs = (
        P("store", None),
        P(None, "ctx", None),
        P("store", "ctx", None),
        P("store", None, "ctx", None),
        P(),
        P(),
        P("store", None),
        P("store"),
        P(("store", "ctx"), None, None),
    )
    out_specs = P("store", "ctx", None)
    return jax.shard_map(body, mesh=mesh, in_specs=in_specs, out_specs=out_specs, check_vma=False)
```
